256 devices in a mesh: row: 32 (over y, z_lo, core), col: 8 (over z_hi, x).
Axes of the slice: x: 4, y: 4, z: 8 (z_hi: 2, z_lo: 4; z = z_hi * 4 + z_lo), core: 2. Of those that a mesh axis runs over, the one named last changes fastest.
Arguments:
- rhs: bfloat16 [2097152, 128], P(('row', 'col')), may hold values from -6 to 6
- leaf_basis: bfloat16 [16384, 64, 256], P(('row', 'col')), may hold values from -0.375 to 0.375
- transfer: bfloat16 [4, 32, 8, 64, 64, 256], P(None, 'row', 'col'), may hold values from -0.375 to 0.375
- ranks: int32 [4, 32, 8, 64], P(None, 'row', 'col'), may hold values from 32 to 64, as said below
- out_basis: bfloat16 [32, 64, 128, 128], P('row'), may hold values from -0.1875 to 0.1875
Outputs:
- result: bfloat16 [262144, 128], P(('row', 'col'))
The draws below stay inside these ranges and needn't reach their ends.
Inputs may be any that keep to these rules, and one draw needn't show every extreme that they name: `ranks`: at every level some block has live rank exactly 64.
All inputs are finite; a program needn't handle non-finite values.
Results may differ from the reference program's by a relative error of at most 0.0014.
Values sent between devices are 32-bit elements; how exact they have to be, the bound alone decides.
No kernel may reach another device: no remote copies, remote signals or barrier semaphores. Data moves between devices by JAX's collectives and lax.ppermute only.
A program may use at most 128 MiB of HBM per device.

```python
import jax
import jax.numpy as jnp
from jax import lax

R = 64
K = 64
LEAF = 128
LEVELS = 4
G = 64
LEAVES = 16384
UNKNOWNS = 2097152
N_ROW = 32
N_COL = 8


def draw_ranks(key, part):
    key = jax.random.fold_in(key, 7)
    first_key, second_key = jax.random.split(key)
    values = jax.random.randint(first_key, (LEVELS, N_ROW, N_COL, G), K // 2, K + 1)
    chosen = jax.random.randint(second_key, (LEVELS, 1, 1, 1), 0, N_ROW * N_COL * G)
    flat_index = (jnp.arange(N_ROW)[:, None, None] * N_COL + jnp.arange(N_COL)[None, :, None]) * G + jnp.arange(G)[None, None, :]
    return jnp.where(flat_index[None] == chosen, K, values).astype(jnp.int32)


def levels(key, extent, cuts, smallest, largest):
    factor_of, own = 1.0, jax.random.fold_in(key, 6)
    for axis_at, shards_of in cuts:
        heights = jnp.exp(jax.random.uniform(jax.random.fold_in(own, axis_at), (shards_of,), jnp.float32, smallest / len(cuts), largest / len(cuts)))
        factor_of = factor_of * jnp.repeat(heights, extent[axis_at] // shards_of).reshape([-1 if axis == axis_at else 1 for axis in range(len(extent))])
    return factor_of


def bell_draw(own_key, extent, width, reach, cuts=(), kind=jnp.bfloat16):
    values = width * jax.random.normal(own_key, extent, jnp.float32)
    if cuts:
        values = values * levels(own_key, extent, cuts, -0.22, 0.18)
    return jnp.clip(values, -reach, reach).astype(kind)


def setup_inputs(seed: int = 0) -> dict:
    streams_of = jax.random.split(jax.random.key(seed), 6)
    return {
        "rhs": bell_draw(streams_of[0], (UNKNOWNS, 2 * R), 1.0, 6.0, ((0, 256),)),
        "leaf_basis": bell_draw(streams_of[1], (LEAVES, K, 2 * LEAF), (2 * LEAF) ** -0.5, 0.375, ((0, 256),)),
        "transfer": bell_draw(streams_of[2], (LEVELS, N_ROW, N_COL, G, K, 4 * K), (4 * K) ** -0.5, 0.375, ((1, 32), (2, 8))),
        "ranks": draw_ranks(jax.random.fold_in(streams_of[5], 71), 0),
        "out_basis": bell_draw(streams_of[4], (N_ROW, G, LEAF, 2 * K), (2 * K * N_COL) ** -0.5, 0.1875, ((0, 32),)),
    }


def complex_stack(block):
    middle = block.shape[-1] // 2
    flipped = jnp.concatenate([-block[..., middle:], block[..., :middle]], -1)
    return jnp.concatenate([block, flipped], -2)


def reference(rhs, leaf_basis, transfer, ranks, out_basis):
    positions = transfer.shape[1]
    columns_count = transfer.shape[2]
    blocks_dev = transfer.shape[3]
    rank_cap = leaf_basis.shape[1]
    points = leaf_basis.shape[2] // 2
    columns = rhs.shape[1]
    half_count = blocks_dev // 2
    sources = rhs.reshape(positions, columns_count * blocks_dev, points, columns)
    bases = leaf_basis.reshape(positions, columns_count * blocks_dev, rank_cap, 2 * points)

    def leaf_apply(pair):
        source, basis = pair
        return jnp.einsum('gkm,gmn->gkn', basis.astype(jnp.float32), complex_stack(source.astype(jnp.float32)), precision=lax.Precision.HIGHEST)

    coeff = lax.map(leaf_apply, (sources, bases))
    coeff = coeff.reshape(positions, columns_count, blocks_dev, rank_cap, columns)
    index = jnp.arange(positions, dtype=jnp.int32)
    for level in range(transfer.shape[0]):
        upper_bit = ((index >> level) & 1)[:, None, None, None, None]
        partner = index ^ (1 << level)
        halves = coeff.reshape(positions, columns_count, 2, half_count, rank_cap, columns)
        kept_half = jnp.where(upper_bit == 1, halves[:, :, 1], halves[:, :, 0])
        other = halves[partner]
        partner_half = jnp.where(upper_bit == 1, other[:, :, 1], other[:, :, 0])
        stacked = jnp.concatenate([complex_stack(kept_half), complex_stack(partner_half)], -2)
        matrices = transfer[level].astype(jnp.float32).reshape(positions, columns_count, half_count, 2, rank_cap, 4 * rank_cap)
        mixed = jnp.einsum('pcjskm,pcjmn->pcjskn', matrices, stacked, precision=lax.Precision.HIGHEST)
        mixed = mixed.reshape(positions, columns_count, blocks_dev, rank_cap, columns)
        live_rows = jnp.arange(rank_cap, dtype=jnp.int32)[None, None, None, :] < ranks[level][..., None]
        coeff = jnp.where(live_rows[..., None], mixed, jnp.float32(0.0))
    total = jnp.sum(coeff, axis=1)
    result = jnp.einsum('pglm,pgmn->pgln', out_basis.astype(jnp.float32), complex_stack(total), precision=lax.Precision.HIGHEST)
    return result.reshape(positions * blocks_dev * points, columns).astype(jnp.bfloat16)
```

```python
import functools

import jax
import jax.numpy as jnp
from jax import lax
from jax.experimental import pallas as pl
from jax.experimental.pallas import tpu as pltpu
from jax.sharding import PartitionSpec as P

SLOTS = 4


def swap(block, axis, mask):
    count = lax.axis_size(axis)
    return lax.ppermute(block, axis, [(at, at ^ mask) for at in range(count)])


def turn(block):
    middle = block.shape[-1] // 2
    return jnp.concatenate([-block[:, middle:], block[:, :middle]], -1)


def split(block):
    high = block.astype(jnp.bfloat16)
    low = (block - high.astype(jnp.float32)).astype(jnp.bfloat16)
    return high, low


def stack_split(blocks):
    highs, lows = [], []
    for block in blocks:
        high, low = split(block)
        highs += [high, turn(high)]
        lows += [low, turn(low)]
    return jnp.concatenate([jnp.concatenate(highs, 0), jnp.concatenate(lows, 0)], 1)


def leaf_kernel(scalars, rhs_ref, basis_ref, sent_ref, kept_ref, *, bit_at):
    half = sent_ref.shape[0]
    bit = scalars[bit_at]
    for out_ref, start in ((sent_ref, (1 - bit) * half), (kept_ref, bit * half)):
        for at in range(half):
            source = rhs_ref[start + at, 0]
            stacked = jnp.concatenate([source, turn(source)], 0)
            out_ref[at] = jnp.dot(
                basis_ref[start + at, 0], stacked, preferred_element_type=jnp.float32
            )


def level_kernel(scalars, ranks, own_ref, partner_ref, matrices_ref, *refs, level, slot, bit_at, leaves):
    sent_ref, kept_ref = refs[-2:]
    added = refs[:-2]
    half = sent_ref.shape[0]
    rank_cap, columns = sent_ref.shape[1:]
    low_count = matrices_ref.shape[3]
    chunk = scalars[slot]
    bit = scalars[bit_at]
    rows = lax.broadcasted_iota(jnp.int32, (rank_cap, columns), 0)
    for which, (out_ref, start) in enumerate(((sent_ref, (1 - bit) * half), (kept_ref, bit * half))):
        for pair in range(half // 2):
            j = start // 2 + pair
            stacked = stack_split([own_ref[j], partner_ref[j]])
            places, parts = [], []
            for s in range(2):
                local = start + 2 * pair + s
                high, low = local // low_count, local % low_count
                places.append(high * (SLOTS * low_count) + chunk * low_count + low)
                parts.append(matrices_ref[0, high, 0, low])
            both = jnp.dot(jnp.concatenate(parts, 0), stacked, preferred_element_type=jnp.float32)
            both = both[:, :columns] + both[:, columns:]
            for s in range(2):
                live = ranks[level * leaves + places[s]]
                mixed = jnp.where(rows < live, both[s * rank_cap : (s + 1) * rank_cap], 0.0)
                if added:
                    mixed = mixed + added[which][2 * pair + s]
                out_ref[2 * pair + s] = mixed


def target_kernel(scalars, basis_ref, first_ref, second_ref, third_ref, out_ref):
    points = basis_ref.shape[2]
    columns = out_ref.shape[1]
    for at in range(first_ref.shape[0]):
        total = first_ref[at] + second_ref[at] + third_ref[at]
        both = jnp.dot(basis_ref[0, at], stack_split([total]), preferred_element_type=jnp.float32)
        out_ref[at * points : (at + 1) * points, :] = (
            both[:, :columns] + both[:, columns:]
        ).astype(out_ref.dtype)


def whole(shape):
    return pl.BlockSpec(shape, lambda step, *_: (0,) * len(shape))


def call(body, prefetch, in_specs, outs, flops, moved):
    return pl.pallas_call(
        body,
        grid_spec=pltpu.PrefetchScalarGridSpec(
            num_scalar_prefetch=prefetch,
            grid=(1,),
            in_specs=in_specs,
            out_specs=[whole(out.shape) for out in outs],
        ),
        out_shape=outs,
        cost_estimate=pl.CostEstimate(flops=flops, bytes_accessed=moved, transcendentals=0),
        compiler_params=pltpu.CompilerParams(vmem_limit_bytes=16 * 1024 * 1024),
    )


def shards(rhs, leaf_basis, transfer, ranks, out_basis):
    leaves, rank_cap, wide = leaf_basis.shape
    points = wide // 2
    columns = rhs.shape[1]
    levels = transfer.shape[0]
    chunk_leaves = leaves // SLOTS
    half = chunk_leaves // 2
    position = lax.axis_index("row")
    column = lax.axis_index("col")
    column_count = lax.axis_size("col")
    owned = leaves // column_count
    scalars = jnp.stack(
        [(column >> 1) ^ (SLOTS - 1 - slot) for slot in range(SLOTS)]
        + [position >> level & 1 for level in range(levels)]
        + [column & 1, column]
    ).astype(jnp.int32)
    flat_ranks = ranks.reshape(levels * leaves)
    sources = rhs.reshape(chunk_leaves, SLOTS, points, columns)
    bases = leaf_basis.reshape(chunk_leaves, SLOTS, rank_cap, wide)
    half_out = jax.ShapeDtypeStruct((half, rank_cap, columns), jnp.float32)
    half_spec = whole(half_out.shape)

    def leaf(slot):
        at_slot = lambda step, scalars: (0, scalars[slot], 0, 0)
        return call(
            functools.partial(leaf_kernel, bit_at=SLOTS),
            1,
            [
                pl.BlockSpec((chunk_leaves, 1, points, columns), at_slot),
                pl.BlockSpec((chunk_leaves, 1, rank_cap, wide), at_slot),
            ],
            [half_out, half_out],
            2 * chunk_leaves * rank_cap * wide * columns,
            3 << 19,
        )(scalars, sources, bases)

    def mix(level, slot, kept, partner, added=()):
        low_count = 2 << level
        high_count = chunk_leaves // low_count
        matrices = transfer.reshape(levels, high_count, SLOTS, low_count, rank_cap, 4 * rank_cap)
        return call(
            functools.partial(
                level_kernel, level=level, slot=slot, bit_at=SLOTS + level + 1, leaves=leaves
            ),
            2,
            [
                half_spec,
                half_spec,
                pl.BlockSpec(
                    (1, high_count, 1, low_count, rank_cap, 4 * rank_cap),
                    lambda step, scalars, ranks: (level, 0, scalars[slot], 0, 0, 0),
                ),
            ]
            + [half_spec] * len(added),
            [half_out, half_out],
            4 * chunk_leaves * rank_cap * 4 * rank_cap * columns,
            3 << 19,
        )(scalars, flat_ranks, kept, partner, matrices, *added)

    def through(slot, added=()):
        sent, kept = leaf(slot)
        for level in range(levels):
            partner = swap(sent, "row", 1 << level)
            sent, kept = mix(level, slot, kept, partner, added if level == levels - 1 else ())
        return sent, kept

    summed = []
    for first in (0, 2):
        sent, kept = through(first)
        added = (swap(kept, "col", 3), swap(sent, "col", 3))
        sent, kept = through(first + 1, added)
        summed.append((kept, swap(sent, "col", 1)))
    far = swap(summed[0][0] + summed[0][1], "col", 4)

    result = call(
        target_kernel,
        1,
        [pl.BlockSpec((1, owned, points, 2 * rank_cap), lambda step, scalars: (0, scalars[SLOTS + levels + 1], 0, 0))]
        + [half_spec] * 3,
        [jax.ShapeDtypeStruct((owned * points, columns), jnp.bfloat16)],
        4 * owned * points * 2 * rank_cap * columns,
        3 << 19,
    )(scalars, out_basis, summed[1][0], summed[1][1], far)
    return result[0]


def solution(mesh):
    in_specs = (
        P(("row", "col"), None),
        P(("row", "col"), None, None),
        P(None, "row", "col", None, None, None),
        P(None, "row", "col", None),
        P("row", None, None, None),
    )
    out_specs = P(("row", "col"), None)
    return jax.shard_map(shards, mesh=mesh, in_specs=in_specs, out_specs=out_specs, check_vma=False)
```

```python
import functools

import jax
import jax.numpy as jnp
from jax import lax
from jax.experimental import pallas as pl
from jax.experimental.pallas import tpu as pltpu
from jax.sharding import PartitionSpec as P

SLOTS = 4

ORDER = [
    ("leaf", 0), ("leaf", 1), ("mix", 0, 0), ("leaf", 2), ("leaf", 3), ("mix", 1, 0),
    ("mix", 0, 1), ("mix", 1, 1), ("mix", 0, 2), ("mix", 2, 0), ("mix", 1, 2), ("mix", 3, 0),
    ("mix", 0, 3), ("mix", 2, 1), ("mix", 1, 3), ("mix", 3, 1), ("mix", 2, 2), ("mix", 3, 2),
    ("mix", 2, 3), ("far",), ("mix", 3, 3), ("end",),
]


def swap(block, axis, mask):
    count = lax.axis_size(axis)
    return lax.ppermute(block, axis, [(at, at ^ mask) for at in range(count)])


def turn(block):
    middle = block.shape[-1] // 2
    return jnp.concatenate([-block[:, middle:], block[:, :middle]], -1)


def split(block):
    high = block.astype(jnp.bfloat16)
    low = (block - high.astype(jnp.float32)).astype(jnp.bfloat16)
    return high, low


def stack_split(blocks):
    highs, lows = [], []
    for block in blocks:
        high, low = split(block)
        highs += [high, turn(high)]
        lows += [low, turn(low)]
    return jnp.concatenate([jnp.concatenate(highs, 0), jnp.concatenate(lows, 0)], 1)


def halves(bit, half):
    return (1 - bit) * half, bit * half


def leaf_body(scalars, ranks, mine, outs, *, bit_at):
    rhs_ref, basis_ref = mine
    half = outs[0].shape[0]
    for out_ref, start in zip(outs, halves(scalars[bit_at], half)):
        for at in range(half):
            source = rhs_ref[start + at]
            stacked = jnp.concatenate([source, turn(source)], 0)
            out_ref[at] = jnp.dot(basis_ref[start + at], stacked, preferred_element_type=jnp.float32)


def mix_body(scalars, ranks, mine, outs, *, level, slot, bit_at):
    matrices_ref, own_ref, partner_ref = mine[:3]
    added = mine[3:]
    half, rank_cap, columns = outs[0].shape
    low_count = 2 << level
    chunk = scalars[slot]
    rows = lax.broadcasted_iota(jnp.int32, (rank_cap, columns), 0)
    for which, (out_ref, start) in enumerate(zip(outs, halves(scalars[bit_at], half))):
        for pair in range(half // 2):
            j = start // 2 + pair
            stacked = stack_split([own_ref[j], partner_ref[j]])
            first = start + 2 * pair
            left = jnp.concatenate([matrices_ref[first], matrices_ref[first + 1]], 0)
            both = jnp.dot(left, stacked, preferred_element_type=jnp.float32)
            both = both[:, :columns] + both[:, columns:]
            for s in range(2):
                local = first + s
                place = (local // low_count) * (SLOTS * low_count) + chunk * low_count + local % low_count
                live = ranks[level, 0, 0, place]
                mixed = jnp.where(rows < live, both[s * rank_cap : (s + 1) * rank_cap], 0.0)
                if added:
                    mixed = mixed + added[which][2 * pair + s]
                out_ref[2 * pair + s] = mixed


def far_body(scalars, ranks, mine, outs):
    for at in range(outs[0].shape[0]):
        outs[0][at] = mine[0][at] + mine[1][at]


def end_body(scalars, ranks, mine, outs):
    basis_ref, first_ref, second_ref, third_ref = mine
    out_ref = outs[0]
    points = basis_ref.shape[1]
    columns = out_ref.shape[1]
    for at in range(first_ref.shape[0]):
        total = first_ref[at] + second_ref[at] + third_ref[at]
        both = jnp.dot(basis_ref[at], stack_split([total]), preferred_element_type=jnp.float32)
        both = both[:, :columns] + both[:, columns:]
        out_ref[at * points : (at + 1) * points, :] = both.astype(out_ref.dtype)


def kernel(*refs, body, sizes, first_copies, next_copies):
    scalars, ranks, token = refs[:3]
    at = 3
    groups = []
    for size in sizes:
        groups.append(refs[at : at + size])
        at += size
    mine, first_from, next_from, outs, next_to, first_to, sems = groups
    loads = list(first_copies(scalars, first_from, first_to, sems[0])) if first_copies else []
    for load in loads:
        load.start()
    coming = list(next_copies(scalars, next_from, next_to, sems[-1])) if next_copies else []
    for load in coming:
        load.start()
    for load in loads:
        load.wait()
    body(scalars, ranks, first_to + mine, outs)
    for load in coming:
        load.wait()


def shards(rhs, leaf_basis, transfer, ranks, out_basis):
    leaves, rank_cap, wide = leaf_basis.shape
    points = wide // 2
    columns = rhs.shape[1]
    levels = transfer.shape[0]
    chunk_leaves = leaves // SLOTS
    half = chunk_leaves // 2
    position = lax.axis_index("row")
    column = lax.axis_index("col")
    column_count = lax.axis_size("col")
    owned = leaves // column_count
    scalars = jnp.stack(
        [(column >> 1) ^ (SLOTS - 1 - slot) for slot in range(SLOTS)]
        + [position >> level & 1 for level in range(levels)]
        + [column & 1, column]
    ).astype(jnp.int32)
    far_memory = lambda array: pltpu.with_memory_space_constraint(array, pltpu.HBM)
    sources = far_memory(rhs.reshape(chunk_leaves, SLOTS, points, columns))
    bases = far_memory(leaf_basis.reshape(chunk_leaves, SLOTS, rank_cap, wide))
    matrices = []
    for level in range(levels):
        low_count = 2 << level
        shape = (levels, chunk_leaves // low_count, SLOTS, low_count, rank_cap, 4 * rank_cap)
        matrices.append(far_memory(transfer.reshape(shape)))
    targets = far_memory(out_basis)
    half_out = ((half, rank_cap, columns), jnp.float32)

    def load_of(step):
        if step[0] == "leaf":
            slot = step[1]

            def copies(scalars, arrays, buffers, sems):
                for at, (array, buffer) in enumerate(zip(arrays, buffers)):
                    yield pltpu.make_async_copy(array.at[:, scalars[slot]], buffer, sems.at[at])

            return [sources, bases], [((chunk_leaves, points, columns), rhs.dtype), ((chunk_leaves, rank_cap, wide), leaf_basis.dtype)], copies, 2
        if step[0] == "mix":
            level, slot = step[1:]
            low_count = 2 << level
            count = chunk_leaves // low_count

            def copies(scalars, arrays, buffers, sems):
                for at in range(count):
                    yield pltpu.make_async_copy(
                        arrays[0].at[level, at, scalars[slot]],
                        buffers[0].at[pl.ds(at * low_count, low_count)],
                        sems.at[at],
                    )

            return [matrices[level]], [((chunk_leaves, rank_cap, 4 * rank_cap), transfer.dtype)], copies, count
        if step[0] == "end":

            def copies(scalars, arrays, buffers, sems):
                yield pltpu.make_async_copy(
                    arrays[0].at[0, pl.ds(scalars[SLOTS + levels + 1] * owned, owned)], buffers[0], sems.at[0]
                )

            return [targets], [((owned, points, 2 * rank_cap), out_basis.dtype)], copies, 1
        return [], [], None, 0

    def run(at, body, loaded, arrays, outs, token, flops):
        first = load_of(ORDER[at]) if at == 0 else ([], [], None, 0)
        after = load_of(ORDER[at + 1]) if at + 1 < len(ORDER) else ([], [], None, 0)
        in_vmem = list(loaded) + [pltpu.with_memory_space_constraint(array, pltpu.VMEM) for array in arrays]
        outs = list(outs)
        last = at + 1 == len(ORDER)
        sems = [count for count in (first[3], after[3]) if count]
        token = [scalars] if token is None else [token]
        sizes = (len(in_vmem), len(first[0]), len(after[0]), len(outs), len(after[1]), len(first[1]), len(sems))
        vmem = pl.BlockSpec(memory_space=pltpu.VMEM)
        smem = pl.BlockSpec(memory_space=pltpu.SMEM)
        anywhere = pl.BlockSpec(memory_space=pl.ANY)
        moved = 4 * sum(array.size for array in arrays) + (3 << 19)
        results = pl.pallas_call(
            functools.partial(kernel, body=body, sizes=sizes, first_copies=first[2], next_copies=after[2]),
            in_specs=[smem, smem, anywhere] + [vmem] * len(in_vmem) + [anywhere] * (len(first[0]) + len(after[0])),
            out_specs=[vmem] * (len(outs) + len(after[1])),
            out_shape=[
                jax.ShapeDtypeStruct(shape, kind) if last else pltpu.VMEM(shape, kind) for shape, kind in outs + after[1]
            ],
            scratch_shapes=[pltpu.VMEM(shape, kind) for shape, kind in first[1]]
            + [pltpu.SemaphoreType.DMA((count,)) for count in sems],
            cost_estimate=pl.CostEstimate(flops=flops, bytes_accessed=moved, transcendentals=0),
            compiler_params=pltpu.CompilerParams(vmem_limit_bytes=16 * 1024 * 1024),
        )(scalars, ranks, *token, *in_vmem, *first[0], *after[0])
        return results[: len(outs)], results[len(outs) :]

    loaded, token = [], None
    sent, kept, added, near = {}, {}, {}, {}
    far = result = None
    for at, step in enumerate(ORDER):
        if step[0] == "leaf":
            slot = step[1]
            body = functools.partial(leaf_body, bit_at=SLOTS)
            flops = 2 * chunk_leaves * rank_cap * wide * columns
            (sent[slot], kept[slot]), loaded = run(at, body, loaded, [], [half_out] * 2, token, flops)
            token = kept[slot]
        elif step[0] == "mix":
            level, slot = step[1:]
            partner = swap(sent[slot], "row", 1 << level)
            body = functools.partial(mix_body, level=level, slot=slot, bit_at=SLOTS + level + 1)
            arrays = [kept[slot], partner] + (added.get(slot, []) if level == levels - 1 else [])
            flops = 4 * chunk_leaves * rank_cap * 4 * rank_cap * columns
            (sent[slot], kept[slot]), loaded = run(at, body, loaded, arrays, [half_out] * 2, token, flops)
            token = kept[slot]
            if level == levels - 1:
                if slot % 2 == 0:
                    added[slot + 1] = [swap(kept[slot], "col", 3), swap(sent[slot], "col", 3)]
                else:
                    near[slot] = swap(sent[slot], "col", 1)
        elif step[0] == "far":
            (total,), loaded = run(at, far_body, loaded, [kept[1], near[1]], [half_out], token, 1 << 16)
            far = swap(total, "col", 4)
            token = total
        else:
            arrays = [kept[3], near[3], far]
            out = ((owned * points, columns), jnp.bfloat16)
            flops = 4 * owned * points * 2 * rank_cap * columns
            (result,), _ = run(at, end_body, loaded, arrays, [out], token, flops)
    return result


def solution(mesh):
    in_specs = (
        P(("row", "col"), None),
        P(("row", "col"), None, None),
        P(None, "row", "col", None, None, None),
        P(None, "row", "col", None),
        P("row", None, None, None),
    )
    out_specs = P(("row", "col"), None)
    return jax.shard_map(shards, mesh=mesh, in_specs=in_specs, out_specs=out_specs, check_vma=False)
```

```python
import functools

import jax
import jax.numpy as jnp
from jax import lax
from jax.experimental import pallas as pl
from jax.experimental.pallas import tpu as pltpu
from jax.sharding import PartitionSpec as P

SLOTS = 4

ORDER = [
    ("first",), ("rest",), ("mix", 0, 0), ("load",), ("mix", 0, 1), ("mix", 1, 0),
    ("mix", 1, 1), ("mix", 0, 2), ("mix", 2, 0), ("mix", 1, 2), ("mix", 3, 0),
    ("mix", 0, 3), ("mix", 2, 1), ("mix", 1, 3), ("mix", 3, 1), ("mix", 2, 2), ("mix", 3, 2),
    ("mix", 2, 3), ("far",), ("mix", 3, 3), ("end",),
]


def swap(block, axis, mask):
    count = lax.axis_size(axis)
    return lax.ppermute(block, axis, [(at, at ^ mask) for at in range(count)])


def turn(block):
    middle = block.shape[-1] // 2
    return jnp.concatenate([-block[:, middle:], block[:, :middle]], -1)


def split(block):
    high = block.astype(jnp.bfloat16)
    low = (block - high.astype(jnp.float32)).astype(jnp.bfloat16)
    return high, low


def stack_split(blocks):
    highs, lows = [], []
    for block in blocks:
        high, low = split(block)
        highs += [high, turn(high)]
        lows += [low, turn(low)]
    return jnp.concatenate([jnp.concatenate(highs, 0), jnp.concatenate(lows, 0)], 1)


def halves(bit, half):
    return (1 - bit) * half, bit * half


def slot_chunk(slot):
    return (lax.axis_index("col") >> 1) ^ (SLOTS - 1 - slot)


def leaf_product(source, basis):
    stacked = jnp.concatenate([source, turn(source)], 0)
    return jnp.dot(basis, stacked, preferred_element_type=jnp.float32)


def first_body(mine, outs, *, half):
    rhs_ref, basis_ref = mine
    sent_ref, kept_ref, rhs_to, basis_to, sems = outs
    chunk = slot_chunk(0)
    starts = halves(level_bit(0), half)
    loads = []
    for which, start in enumerate(starts):
        for array, to in ((rhs_ref, rhs_to), (basis_ref, basis_to)):
            load = pltpu.make_async_copy(array.at[pl.ds(start, half), chunk], to.at[which], sems.at[len(loads)])
            load.start()
            loads.append(load)
    for which, out_ref in enumerate((sent_ref, kept_ref)):
        loads[2 * which].wait()
        loads[2 * which + 1].wait()
        for at in range(half):
            out_ref[at] = leaf_product(rhs_to[which, at], basis_to[which, at])


def rest_body(mine, outs, *, half):
    rhs_ref, basis_ref, matrices_ref, ranks_ref = mine
    count = 2 * (SLOTS - 1)
    to_refs, live_ref, matrices_to = outs[:count], outs[count], outs[count + 1]
    rhs_to, basis_to, ranks_to, sems = outs[count + 2 :]
    starts = halves(level_bit(0), half)
    ranks_load = pltpu.make_async_copy(ranks_ref, ranks_to, sems.at[0])
    ranks_load.start()
    loads = []
    for slot in range(1, SLOTS):
        chunk = slot_chunk(slot)
        for at, (array, to) in enumerate(((rhs_ref, rhs_to), (basis_ref, basis_to))):
            load = pltpu.make_async_copy(array.at[:, chunk], to.at[slot - 1], sems.at[2 * slot + at])
            load.start()
            loads.append(load)
    matrices_load = pltpu.make_async_copy(matrices_ref.at[0], matrices_to, sems.at[1])
    matrices_load.start()
    ranks_load.wait()
    levels, leaves, columns = live_ref.shape
    diagonal = lax.broadcasted_iota(jnp.int32, (leaves, leaves), 0) == lax.broadcasted_iota(jnp.int32, (leaves, leaves), 1)
    for level in range(levels):
        spread = jnp.broadcast_to(ranks_to[level, 0], (leaves, leaves)).astype(jnp.float32)
        column = jnp.sum(jnp.where(diagonal, spread, 0.0), axis=1, keepdims=True)
        live_ref[level] = jnp.broadcast_to(column, (leaves, columns)).astype(jnp.int32)
    for slot in range(1, SLOTS):
        loads[2 * slot - 2].wait()
        loads[2 * slot - 1].wait()
        for which, start in enumerate(starts):
            for at in range(half):
                product = leaf_product(rhs_to[slot - 1, start + at], basis_to[slot - 1, start + at])
                to_refs[2 * slot - 2 + which][at] = product
    matrices_load.wait()


def load_body(mine, outs):
    matrices_ref, targets_ref = mine
    tos, targets_to, sems = outs[:-2], outs[-2], outs[-1]
    owned = targets_to.shape[0]
    start = lax.axis_index("col") * owned
    loads = [
        pltpu.make_async_copy(matrices_ref.at[level + 1], to, sems.at[level]) for level, to in enumerate(tos)
    ]
    loads.append(pltpu.make_async_copy(targets_ref.at[0, pl.ds(start, owned)], targets_to, sems.at[len(tos)]))
    for load in loads:
        load.start()
    for load in loads:
        load.wait()


def mix_body(mine, outs, *, level, slot, bit):
    live_ref, matrices_ref, own_ref, partner_ref = mine[:4]
    added = mine[4:]
    half, rank_cap, columns = outs[0].shape
    low_count = 2 << level
    chunk = slot_chunk(slot)
    rows = lax.broadcasted_iota(jnp.int32, (rank_cap, columns), 0)
    for which, (out_ref, start) in enumerate(zip(outs, halves(bit(), half))):
        for pair in range(half // 2):
            j = start // 2 + pair
            stacked = stack_split([own_ref[j], partner_ref[j]])
            first = start + 2 * pair
            place = (first // low_count) * (SLOTS * low_count) + chunk * low_count + first % low_count
            left = jnp.concatenate([matrices_ref[place], matrices_ref[place + 1]], 0)
            both = jnp.dot(left, stacked, preferred_element_type=jnp.float32)
            both = both[:, :columns] + both[:, columns:]
            for s in range(2):
                live = live_ref[level, pl.ds(place + s, 1), :]
                mixed = jnp.where(rows < live, both[s * rank_cap : (s + 1) * rank_cap], 0.0)
                if added:
                    mixed = mixed + added[which][2 * pair + s]
                out_ref[2 * pair + s] = mixed


def far_body(mine, outs):
    for at in range(outs[0].shape[0]):
        outs[0][at] = mine[0][at] + mine[1][at]


def end_body(mine, outs):
    basis_ref, first_ref, second_ref, third_ref = mine
    out_ref = outs[0]
    points = basis_ref.shape[1]
    columns = out_ref.shape[1]
    owned = first_ref.shape[0]
    for at in range(owned):
        total = first_ref[at] + second_ref[at] + third_ref[at]
        both = jnp.dot(basis_ref[at], stack_split([total]), preferred_element_type=jnp.float32)
        both = both[:, :columns] + both[:, columns:]
        out_ref[at * points : (at + 1) * points, :] = both.astype(out_ref.dtype)


def kernel(*refs, body, ins):
    body(refs[1 : 1 + ins], refs[1 + ins :])


def level_bit(level):
    return lax.axis_index("row") >> level & 1


def owner_bit():
    return lax.axis_index("col") & 1


def shards(rhs, leaf_basis, transfer, ranks, out_basis):
    leaves, rank_cap, wide = leaf_basis.shape
    points = wide // 2
    columns = rhs.shape[1]
    levels = transfer.shape[0]
    chunk_leaves = leaves // SLOTS
    half = chunk_leaves // 2
    owned = leaves // lax.axis_size("col")
    in_vmem = lambda array: pltpu.with_memory_space_constraint(array, pltpu.VMEM)
    in_hbm = lambda array: pltpu.with_memory_space_constraint(array, pltpu.HBM)
    sources = in_hbm(rhs.reshape(chunk_leaves, SLOTS, points, columns))
    bases = in_hbm(leaf_basis.reshape(chunk_leaves, SLOTS, rank_cap, wide))
    transfers = in_hbm(transfer.reshape(levels, leaves, rank_cap, 4 * rank_cap))
    half_out = ((half, rank_cap, columns), jnp.float32)
    level_out = ((leaves, rank_cap, 4 * rank_cap), transfer.dtype)

    def run(name, body, arrays, outs, token, scratch=(), from_hbm=False, last=False):
        vmem = pl.BlockSpec(memory_space=pltpu.VMEM)
        anywhere = pl.BlockSpec(memory_space=pl.ANY)
        if not from_hbm:
            arrays = [in_vmem(array) for array in arrays]
        return pl.pallas_call(
            functools.partial(kernel, body=body, ins=len(arrays)),
            in_specs=[anywhere] + [anywhere if from_hbm else vmem] * len(arrays),
            out_specs=[vmem] * len(outs),
            out_shape=[jax.ShapeDtypeStruct(*out) if last else pltpu.VMEM(*out) for out in outs],
            scratch_shapes=scratch,
            cost_estimate=pl.CostEstimate(flops=1 << 33, bytes_accessed=1 << 20, transcendentals=0),
            compiler_params=pltpu.CompilerParams(vmem_limit_bytes=16 * 1024 * 1024),
            name=name,
        )(token, *arrays)

    token = transfers
    sent, kept, added, near = {}, {}, {}, {}
    live = far = targets = result = None
    matrices = []
    for step in ORDER:
        name = "_".join(str(part) for part in step)
        if step[0] == "first":
            scratch = [
                pltpu.VMEM((2, half, points, columns), rhs.dtype),
                pltpu.VMEM((2, half, rank_cap, wide), leaf_basis.dtype),
                pltpu.SemaphoreType.DMA((4,)),
            ]
            body = functools.partial(first_body, half=half)
            sent[0], kept[0] = run(name, body, [sources, bases], [half_out] * 2, token, scratch, True)
            token = kept[0]
        elif step[0] == "rest":
            scratch = [
                pltpu.VMEM((SLOTS - 1, chunk_leaves, points, columns), rhs.dtype),
                pltpu.VMEM((SLOTS - 1, chunk_leaves, rank_cap, wide), leaf_basis.dtype),
                pltpu.VMEM(ranks.shape, ranks.dtype),
                pltpu.SemaphoreType.DMA((2 * SLOTS,)),
            ]
            outs = [half_out] * (2 * SLOTS - 2) + [((levels, leaves, columns), jnp.int32), level_out]
            body = functools.partial(rest_body, half=half)
            made = run(name, body, [sources, bases, transfers, in_hbm(ranks)], outs, token, scratch, True)
            for slot in range(1, SLOTS):
                sent[slot], kept[slot] = made[2 * slot - 2 : 2 * slot]
            live, first_matrices = made[-2:]
            matrices = [first_matrices]
            token = live
        elif step[0] == "load":
            outs = [level_out] * (levels - 1) + [((owned, points, 2 * rank_cap), out_basis.dtype)]
            scratch = [pltpu.SemaphoreType.DMA((levels,))]
            made = run(name, load_body, [transfers, in_hbm(out_basis)], outs, token, scratch, True)
            matrices += made[:-1]
            token = targets = made[-1]
        elif step[0] == "mix":
            level, slot = step[1:]
            last = level == levels - 1
            partner = swap(sent[slot], "row", 1 << level)
            bit = owner_bit if last else functools.partial(level_bit, level + 1)
            body = functools.partial(mix_body, level=level, slot=slot, bit=bit)
            arrays = [live, matrices[level], kept[slot], partner] + (added.get(slot, []) if last else [])
            sent[slot], kept[slot] = run(name, body, arrays, [half_out] * 2, token)
            token = kept[slot]
            if last and slot % 2 == 0:
                added[slot + 1] = [swap(kept[slot], "col", 3), swap(sent[slot], "col", 3)]
            elif last:
                near[slot] = swap(sent[slot], "col", 1)
        elif step[0] == "far":
            (total,) = run(name, far_body, [kept[1], near[1]], [half_out], token)
            far = swap(total, "col", 4)
            token = total
        else:
            out = ((owned * points, columns), jnp.bfloat16)
            (result,) = run(name, end_body, [targets, kept[3], near[3], far], [out], token, last=True)
    return result


def solution(mesh):
    in_specs = (
        P(("row", "col"), None),
        P(("row", "col"), None, None),
        P(None, "row", "col", None, None, None),
        P(None, "row", "col", None),
        P("row", None, None, None),
    )
    out_specs = P(("row", "col"), None)
    return jax.shard_map(shards, mesh=mesh, in_specs=in_specs, out_specs=out_specs, check_vma=False)
```

```python
import functools

import jax
import jax.numpy as jnp
from jax import lax
from jax.experimental import pallas as pl
from jax.experimental.pallas import tpu as pltpu
from jax.sharding import PartitionSpec as P

SLOTS = 4
LEVELS = 4

ORDER = [
    ('first',),
    ('tables',),
    ('mix', 0, 0, ('sent_a', 'sent_b', 'kept')),
    ('rest',),
    ('mix', 1, 0, ('sent',)),
    ('mix', 1, 0, ('kept',)),
    ('mix', 0, 1, ('sent', 'kept')),
    ('load',),
    ('mix', 1, 1, ('sent', 'kept')),
    ('mix', 0, 2, ('sent', 'kept')),
    ('mix', 2, 0, ('sent', 'kept')),
    ('mix', 0, 3, ('sent', 'kept'), 2),
    ('mix', 1, 2, ('sent', 'kept')),
    ('mix', 3, 0, ('kept_sent',)),
    ('mix', 2, 1, ('sent', 'kept')),
    ('mix', 1, 3, ('sent_a', 'sent_b', 'kept')),
    ('mix', 2, 2, ('sent', 'kept')),
    ('mix', 3, 1, ('sent', 'kept')),
    ('mix', 2, 3, ('sent',)),
    ('mix', 3, 2, ('kept',)),
    ('far',),
    ('mix', 2, 3, ('kept',)),
    ('mix', 3, 2, ('sent',)),
    ('targets',),
    ('mix', 3, 3, ('sent',)),
    ('mix', 3, 3, ('kept',)),
    ('end',),
]


def swap(block, axis, mask):
    count = lax.axis_size(axis)
    return lax.ppermute(block, axis, [(at, at ^ mask) for at in range(count)])


def turn(block):
    middle = block.shape[-1] // 2
    return jnp.concatenate([-block[:, middle:], block[:, :middle]], -1)


def split(block):
    high = block.astype(jnp.bfloat16)
    low = (block - high.astype(jnp.float32)).astype(jnp.bfloat16)
    return high, low


def stack_split(blocks):
    highs, lows = [], []
    for block in blocks:
        high, low = split(block)
        highs += [high, turn(high)]
        lows += [low, turn(low)]
    return jnp.concatenate([jnp.concatenate(highs, 0), jnp.concatenate(lows, 0)], 1)


def halves(bit, half):
    return (1 - bit) * half, bit * half


def piece_range(piece, level, half):
    bit = owner_bit() if level == LEVELS - 1 else level_bit(level + 1)
    sent, kept = halves(bit, half)
    if piece == "kept":
        return kept, half
    if piece == "sent":
        return sent, half
    first, second = halves(level_bit(level + 2), half // 2)
    return sent + (first if piece == "sent_a" else second), half // 2


def slot_chunk(slot):
    return (lax.axis_index("col") >> 1) ^ (SLOTS - 1 - slot)


def leaf_product(source, basis):
    stacked = jnp.concatenate([source, turn(source)], 0)
    return jnp.dot(basis, stacked, preferred_element_type=jnp.float32)


def first_body(mine, outs, *, half):
    rhs_ref, basis_ref = mine
    sent_ref, kept_ref, rhs_to, basis_to, sems = outs
    chunk = slot_chunk(0)
    starts = halves(level_bit(0), half)
    loads = []
    for which, start in enumerate(starts):
        for array, to in ((rhs_ref, rhs_to), (basis_ref, basis_to)):
            load = pltpu.make_async_copy(array.at[pl.ds(start, half), chunk], to.at[which], sems.at[len(loads)])
            load.start()
            loads.append(load)
    for which, out_ref in enumerate((sent_ref, kept_ref)):
        loads[2 * which].wait()
        loads[2 * which + 1].wait()
        for at in range(half):
            out_ref[at] = leaf_product(rhs_to[which, at], basis_to[which, at])


def tables_body(mine, outs):
    matrices_ref, ranks_ref = mine
    live_ref, matrices_to, ranks_to, sems = outs
    ranks_load = pltpu.make_async_copy(ranks_ref, ranks_to, sems.at[0])
    ranks_load.start()
    matrices_load = pltpu.make_async_copy(matrices_ref.at[0], matrices_to, sems.at[1])
    matrices_load.start()
    ranks_load.wait()
    levels, leaves, columns = live_ref.shape
    diagonal = lax.broadcasted_iota(jnp.int32, (leaves, leaves), 0) == lax.broadcasted_iota(jnp.int32, (leaves, leaves), 1)
    for level in range(levels):
        spread = jnp.broadcast_to(ranks_to[level, 0], (leaves, leaves)).astype(jnp.float32)
        column = jnp.sum(jnp.where(diagonal, spread, 0.0), axis=1, keepdims=True)
        live_ref[level] = jnp.broadcast_to(column, (leaves, columns)).astype(jnp.int32)
    matrices_load.wait()


def rest_body(mine, outs, *, half):
    rhs_ref, basis_ref, matrices_ref = mine
    sent_ref, kept_ref, matrices_to, rhs_to, basis_to, sems = outs
    starts = halves(level_bit(0), half)
    loads = []
    for slot in range(1, SLOTS):
        chunk = slot_chunk(slot)
        for at, (array, to) in enumerate(((rhs_ref, rhs_to), (basis_ref, basis_to))):
            load = pltpu.make_async_copy(array.at[:, chunk], to.at[slot - 1], sems.at[2 * slot + at])
            load.start()
            loads.append(load)
    matrices_load = pltpu.make_async_copy(matrices_ref.at[1], matrices_to, sems.at[0])
    matrices_load.start()
    for slot in range(1, SLOTS):
        loads[2 * slot - 2].wait()
        loads[2 * slot - 1].wait()
        for to_ref, start in zip((sent_ref, kept_ref), starts):
            for at in range(half):
                product = leaf_product(rhs_to[slot - 1, start + at], basis_to[slot - 1, start + at])
                to_ref[(slot - 1) * half + at] = product
    matrices_load.wait()


def load_body(mine, outs):
    tos, sems = outs[:-1], outs[-1]
    loads = [
        pltpu.make_async_copy(mine[0].at[level + 2], to, sems.at[level]) for level, to in enumerate(tos)
    ]
    for load in loads:
        load.start()
    for load in loads:
        load.wait()


def targets_body(mine, outs):
    to, sem = outs
    owned = to.shape[0]
    load = pltpu.make_async_copy(mine[0].at[0, pl.ds(lax.axis_index("col") * owned, owned)], to, sem)
    load.start()
    load.wait()


def mix_body(mine, outs, *, level, slot, pieces, half, offset, in_parts):
    live_ref, matrices_ref, own_ref, partner_ref = mine[:4]
    added = mine[4:]
    rank_cap, columns = outs[0].shape[1:]
    low_count = 2 << level
    chunk = slot_chunk(slot)
    rows = lax.broadcasted_iota(jnp.int32, (rank_cap, columns), 0)
    if pieces == ("kept_sent",):
        pieces, outs = ("kept", "sent"), (outs[0].at[pl.ds(0, half)], outs[0].at[pl.ds(half, half)])
    for piece, out_ref in zip(pieces, outs):
        start, count = piece_range(piece, level, half)
        for pair in range(count // 2):
            j = start // 2 + pair
            partner = partner_ref[pair if in_parts else offset + j]
            stacked = stack_split([own_ref[offset + j], partner])
            first = start + 2 * pair
            place = (first // low_count) * (SLOTS * low_count) + chunk * low_count + first % low_count
            left = jnp.concatenate([matrices_ref[place], matrices_ref[place + 1]], 0)
            both = jnp.dot(left, stacked, preferred_element_type=jnp.float32)
            both = both[:, :columns] + both[:, columns:]
            for s in range(2):
                live = live_ref[level, pl.ds(place + s, 1), :]
                mixed = jnp.where(rows < live, both[s * rank_cap : (s + 1) * rank_cap], 0.0)
                if added and added[0].shape[0] > half:
                    mixed = mixed + added[0][(half if piece == "kept" else 0) + 2 * pair + s]
                elif added:
                    mixed = mixed + added[0][2 * pair + s]
                out_ref[2 * pair + s] = mixed


def far_body(mine, outs):
    for at in range(outs[0].shape[0]):
        outs[0][at] = mine[0][at] + mine[1][at]


def end_body(mine, outs):
    basis_ref, *summed = mine
    out_ref = outs[0]
    points = basis_ref.shape[1]
    columns = out_ref.shape[1]
    for at in range(basis_ref.shape[0]):
        total = summed[0][at]
        for other in summed[1:]:
            total = total + other[at]
        both = jnp.dot(basis_ref[at], stack_split([total]), preferred_element_type=jnp.float32)
        both = both[:, :columns] + both[:, columns:]
        out_ref[at * points : (at + 1) * points, :] = both.astype(out_ref.dtype)


def kernel(*refs, body, first, ins):
    body(refs[first : first + ins], refs[first + ins :])


def level_bit(level):
    return lax.axis_index("row") >> level & 1


def owner_bit():
    return lax.axis_index("col") & 1


def shards(rhs, leaf_basis, transfer, ranks, out_basis):
    leaves, rank_cap, wide = leaf_basis.shape
    points = wide // 2
    columns = rhs.shape[1]
    levels = transfer.shape[0]
    chunk_leaves = leaves // SLOTS
    half = chunk_leaves // 2
    owned = leaves // lax.axis_size("col")
    in_vmem = lambda array: pltpu.with_memory_space_constraint(array, pltpu.VMEM)
    in_hbm = lambda array: pltpu.with_memory_space_constraint(array, pltpu.HBM)
    sources = in_hbm(rhs.reshape(chunk_leaves, SLOTS, points, columns))
    bases = in_hbm(leaf_basis.reshape(chunk_leaves, SLOTS, rank_cap, wide))
    transfers = in_hbm(transfer.reshape(levels, leaves, rank_cap, 4 * rank_cap))
    half_out = ((half, rank_cap, columns), jnp.float32)
    level_out = ((leaves, rank_cap, 4 * rank_cap), transfer.dtype)

    def run(name, body, arrays, outs, token, scratch=(), from_hbm=False, last=False):
        token = token if isinstance(token, tuple) else (token,)
        vmem = pl.BlockSpec(memory_space=pltpu.VMEM)
        anywhere = pl.BlockSpec(memory_space=pl.ANY)
        if not from_hbm:
            arrays = [in_vmem(array) for array in arrays]
        return pl.pallas_call(
            functools.partial(kernel, body=body, first=len(token), ins=len(arrays)),
            in_specs=[anywhere] * len(token) + [anywhere if from_hbm else vmem] * len(arrays),
            out_specs=[vmem] * len(outs),
            out_shape=[jax.ShapeDtypeStruct(*out) if last else pltpu.VMEM(*out) for out in outs],
            scratch_shapes=scratch,
            cost_estimate=pl.CostEstimate(flops=1 << 33, bytes_accessed=1 << 20, transcendentals=0),
            compiler_params=pltpu.CompilerParams(vmem_limit_bytes=16 * 1024 * 1024),
            name=name,
        )(*token, *arrays)

    token = transfers
    kept, arrived, added, near, offset = {}, {}, {}, {}, {}
    live = far = targets = result = None
    matrices, coming = [], {}
    for step in ORDER:
        name = "_".join(str(part) for part in step[:3])
        if step[0] == "first":
            scratch = [
                pltpu.VMEM((2, half, points, columns), rhs.dtype),
                pltpu.VMEM((2, half, rank_cap, wide), leaf_basis.dtype),
                pltpu.SemaphoreType.DMA((4,)),
            ]
            body = functools.partial(first_body, half=half)
            sent, kept[0] = run(name, body, [sources, bases], [half_out] * 2, token, scratch, True)
            arrived[0] = {"sent": swap(sent, "row", 1)}
            offset[0] = 0
            token = kept[0]
        elif step[0] == "tables":
            scratch = [pltpu.VMEM(ranks.shape, ranks.dtype), pltpu.SemaphoreType.DMA((2,))]
            outs = [((levels, leaves, columns), jnp.int32), level_out]
            live, made = run(name, tables_body, [transfers, in_hbm(ranks)], outs, token, scratch, True)
            matrices.append(made)
            token = live
        elif step[0] == "rest":
            scratch = [
                pltpu.VMEM((SLOTS - 1, chunk_leaves, points, columns), rhs.dtype),
                pltpu.VMEM((SLOTS - 1, chunk_leaves, rank_cap, wide), leaf_basis.dtype),
                pltpu.SemaphoreType.DMA((2 * SLOTS,)),
            ]
            outs = [(((SLOTS - 1) * half, rank_cap, columns), jnp.float32)] * 2 + [level_out]
            body = functools.partial(rest_body, half=half)
            sent, token, made = run(name, body, [sources, bases, transfers], outs, token, scratch, True)
            matrices.append(made)
            sent = {"sent": swap(sent, "row", 1)}
            for slot in range(1, SLOTS):
                kept[slot], arrived[slot], offset[slot] = token, sent, (slot - 1) * half
        elif step[0] == "load":
            scratch = [pltpu.SemaphoreType.DMA((levels - 2,))]
            matrices += run(name, load_body, [transfers], [level_out] * (levels - 2), token, scratch, True)
            token = matrices[-1]
        elif step[0] == "targets":
            outs = [((owned, points, 2 * rank_cap), out_basis.dtype)]
            (targets,) = run(name, targets_body, [in_hbm(out_basis)], outs, token, [pltpu.SemaphoreType.DMA], True)
            token = targets
        elif step[0] == "mix":
            level, slot, pieces = step[1:4]
            if step[4:]:
                token = (token, arrived[step[4]]["sent"])
            last = level == levels - 1
            in_parts = "sent" not in arrived[slot]
            partner = arrived[slot]["sent_a" if pieces == ("sent",) else "sent_b"] if in_parts else arrived[slot]["sent"]
            body = functools.partial(
                mix_body, level=level, slot=slot, pieces=pieces, half=half, offset=offset[slot], in_parts=in_parts
            )
            plus = [added[slot, "sent"]] if last and slot % 2 and "sent" in pieces else []
            counts = {"kept_sent": 2 * half, "sent_a": half // 2, "sent_b": half // 2}
            outs = [((counts.get(piece, half), rank_cap, columns), jnp.float32) for piece in pieces]
            made = dict(zip(pieces, run(name, body, [live, matrices[level], kept[slot], partner] + plus, outs, token)))
            token = made[pieces[-1]]
            if last and slot % 2 == 0:
                for piece, other in (("kept", "sent"), ("sent", "kept"), ("kept_sent", "sent")):
                    if piece in made:
                        added[slot + 1, other] = swap(made[piece], "col", 3)
            elif last:
                if "sent" in made:
                    near[slot] = swap(made["sent"], "col", 1)
                if "kept" in made:
                    kept[slot] = made["kept"]
            else:
                coming.setdefault((level, slot), {}).update(
                    {piece: swap(made[piece], "row", 2 << level) for piece in pieces if piece != "kept"}
                )
                if "kept" in made:
                    kept[slot], arrived[slot], offset[slot] = made["kept"], coming[level, slot], 0
        elif step[0] == "far":
            (token,) = run(name, far_body, [kept[1], near[1]], [half_out], token)
            far = swap(token, "col", 4)
        else:
            out = ((owned * points, columns), jnp.bfloat16)
            arrays = [targets, kept[3], added[3, "kept"], near[3], far]
            (result,) = run(name, end_body, arrays, [out], token, last=True)
    return result


def solution(mesh):
    in_specs = (
        P(("row", "col"), None),
        P(("row", "col"), None, None),
        P(None, "row", "col", None, None, None),
        P(None, "row", "col", None),
        P("row", None, None, None),
    )
    out_specs = P(("row", "col"), None)
    return jax.shard_map(shards, mesh=mesh, in_specs=in_specs, out_specs=out_specs, check_vma=False)
```

```python
import functools

import jax
import jax.numpy as jnp
from jax import lax
from jax.experimental import pallas as pl
from jax.experimental.pallas import tpu as pltpu
from jax.sharding import PartitionSpec as P

SLOTS = 4
LEVELS = 4

ORDER = [
    ('first',),
    ('tables',),
    ('mix', 0, 0, ('sent', 'kept')),
    ('rest',),
    ('load',),
    ('mix', 0, 1, ('sent', 'kept')),
    ('mix', 1, 0, ('sent', 'kept')),
    ('mix', 1, 1, ('sent', 'kept')),
    ('mix', 0, 2, ('sent', 'kept')),
    ('mix', 2, 0, ('sent', 'kept')),
    ('mix', 1, 2, ('sent_a', 'sent_b', 'kept')),
    ('mix', 0, 3, ('sent', 'kept')),
    ('mix', 2, 1, ('sent', 'kept')),
    ('mix', 3, 0, ('kept_sent',)),
    ('mix', 3, 1, ('sent', 'kept')),
    ('mix', 2, 2, ('sent',)),
    ('mix', 1, 3, ('sent', 'kept')),
    ('mix', 2, 2, ('kept',)),
    ('mix', 3, 2, ('kept',)),
    ('mix', 2, 3, ('sent', 'kept')),
    ('far',),
    ('mix', 3, 2, ('sent',)),
    ('mix', 3, 3, ('sent',)),
    ('mix', 3, 3, ('kept',)),
    ('targets',),
    ('end',),
]


def swap(block, axis, mask):
    count = lax.axis_size(axis)
    return lax.ppermute(block, axis, [(at, at ^ mask) for at in range(count)])


def turn(block):
    middle = block.shape[-1] // 2
    return jnp.concatenate([-block[:, middle:], block[:, :middle]], -1)


def split(block):
    high = block.astype(jnp.bfloat16)
    low = (block - high.astype(jnp.float32)).astype(jnp.bfloat16)
    return high, low


def stack_split(blocks):
    highs, lows = [], []
    for block in blocks:
        high, low = split(block)
        highs += [high, turn(high)]
        lows += [low, turn(low)]
    return jnp.concatenate([jnp.concatenate(highs, 0), jnp.concatenate(lows, 0)], 1)


def halves(bit, half):
    return (1 - bit) * half, bit * half


def piece_range(piece, level, half):
    bit = owner_bit() if level == LEVELS - 1 else level_bit(level + 1)
    sent, kept = halves(bit, half)
    if piece == "kept":
        return kept, half
    if piece == "sent":
        return sent, half
    first, second = halves(level_bit(level + 2), half // 2)
    return sent + (first if piece == "sent_a" else second), half // 2


def slot_chunk(slot):
    return (lax.axis_index("col") >> 1) ^ (SLOTS - 1 - slot)


def leaf_product(source, basis):
    stacked = jnp.concatenate([source, turn(source)], 0)
    return jnp.dot(basis, stacked, preferred_element_type=jnp.float32)


def first_body(mine, outs, *, half):
    rhs_ref, basis_ref = mine
    sent_ref, kept_ref, rhs_to, basis_to, sems = outs
    chunk = slot_chunk(0)
    starts = halves(level_bit(0), half)
    loads = []
    for which, start in enumerate(starts):
        for array, to in ((rhs_ref, rhs_to), (basis_ref, basis_to)):
            load = pltpu.make_async_copy(array.at[pl.ds(start, half), chunk], to.at[which], sems.at[len(loads)])
            load.start()
            loads.append(load)
    for which, out_ref in enumerate((sent_ref, kept_ref)):
        loads[2 * which].wait()
        loads[2 * which + 1].wait()
        for at in range(half):
            out_ref[at] = leaf_product(rhs_to[which, at], basis_to[which, at])


def tables_body(mine, outs):
    matrices_ref, ranks_ref = mine
    live_ref, matrices_to, ranks_to, sems = outs
    ranks_load = pltpu.make_async_copy(ranks_ref, ranks_to, sems.at[0])
    ranks_load.start()
    matrices_load = pltpu.make_async_copy(matrices_ref.at[0], matrices_to, sems.at[1])
    matrices_load.start()
    ranks_load.wait()
    levels, leaves, columns = live_ref.shape
    diagonal = lax.broadcasted_iota(jnp.int32, (leaves, leaves), 0) == lax.broadcasted_iota(jnp.int32, (leaves, leaves), 1)
    for level in range(levels):
        spread = jnp.broadcast_to(ranks_to[level, 0], (leaves, leaves)).astype(jnp.float32)
        column = jnp.sum(jnp.where(diagonal, spread, 0.0), axis=1, keepdims=True)
        live_ref[level] = jnp.broadcast_to(column, (leaves, columns)).astype(jnp.int32)
    matrices_load.wait()


def rest_body(mine, outs, *, half):
    rhs_ref, basis_ref, matrices_ref = mine
    sent_ref, kept_ref, matrices_to, rhs_to, basis_to, sems = outs
    starts = halves(level_bit(0), half)
    loads = []
    for slot in range(1, SLOTS):
        chunk = slot_chunk(slot)
        for at, (array, to) in enumerate(((rhs_ref, rhs_to), (basis_ref, basis_to))):
            load = pltpu.make_async_copy(array.at[:, chunk], to.at[slot - 1], sems.at[2 * slot + at])
            load.start()
            loads.append(load)
    matrices_load = pltpu.make_async_copy(matrices_ref.at[1], matrices_to, sems.at[0])
    matrices_load.start()
    for slot in range(1, SLOTS):
        loads[2 * slot - 2].wait()
        loads[2 * slot - 1].wait()
        for to_ref, start in zip((sent_ref, kept_ref), starts):
            for at in range(half):
                product = leaf_product(rhs_to[slot - 1, start + at], basis_to[slot - 1, start + at])
                to_ref[(slot - 1) * half + at] = product
    matrices_load.wait()


def load_body(mine, outs):
    tos, sems = outs[:-1], outs[-1]
    loads = [
        pltpu.make_async_copy(mine[0].at[level + 2], to, sems.at[level]) for level, to in enumerate(tos)
    ]
    for load in loads:
        load.start()
    for load in loads:
        load.wait()


def targets_body(mine, outs):
    to, sem = outs
    owned = to.shape[0]
    load = pltpu.make_async_copy(mine[0].at[0, pl.ds(lax.axis_index("col") * owned, owned)], to, sem)
    load.start()
    load.wait()


def mix_body(mine, outs, *, level, slot, pieces, half, offset, in_parts):
    live_ref, matrices_ref, own_ref, partner_ref = mine[:4]
    added = mine[4:]
    rank_cap, columns = outs[0].shape[1:]
    low_count = 2 << level
    chunk = slot_chunk(slot)
    rows = lax.broadcasted_iota(jnp.int32, (rank_cap, columns), 0)
    if pieces == ("kept_sent",):
        pieces, outs = ("kept", "sent"), (outs[0].at[pl.ds(0, half)], outs[0].at[pl.ds(half, half)])
    for piece, out_ref in zip(pieces, outs):
        start, count = piece_range(piece, level, half)
        for pair in range(count // 2):
            j = start // 2 + pair
            partner = partner_ref[pair if in_parts else offset + j]
            stacked = stack_split([own_ref[offset + j], partner])
            first = start + 2 * pair
            place = (first // low_count) * (SLOTS * low_count) + chunk * low_count + first % low_count
            left = jnp.concatenate([matrices_ref[place], matrices_ref[place + 1]], 0)
            both = jnp.dot(left, stacked, preferred_element_type=jnp.float32)
            both = both[:, :columns] + both[:, columns:]
            for s in range(2):
                live = live_ref[level, pl.ds(place + s, 1), :]
                mixed = jnp.where(rows < live, both[s * rank_cap : (s + 1) * rank_cap], 0.0)
                if added and added[0].shape[0] > half:
                    mixed = mixed + added[0][(half if piece == "kept" else 0) + 2 * pair + s]
                elif added:
                    mixed = mixed + added[0][2 * pair + s]
                out_ref[2 * pair + s] = mixed


def far_body(mine, outs):
    for at in range(outs[0].shape[0]):
        total = mine[0][at]
        for other in mine[1:]:
            total = total + other[at]
        outs[0][at] = total


def end_body(mine, outs):
    basis_ref, *summed = mine
    out_ref = outs[0]
    points = basis_ref.shape[1]
    columns = out_ref.shape[1]
    for at in range(basis_ref.shape[0]):
        total = summed[0][at]
        for other in summed[1:]:
            total = total + other[at]
        both = jnp.dot(basis_ref[at], stack_split([total]), preferred_element_type=jnp.float32)
        both = both[:, :columns] + both[:, columns:]
        out_ref[at * points : (at + 1) * points, :] = both.astype(out_ref.dtype)


def kernel(*refs, body, first, ins):
    body(refs[first : first + ins], refs[first + ins :])


def level_bit(level):
    return lax.axis_index("row") >> level & 1


def owner_bit():
    return lax.axis_index("col") & 1


def shards(rhs, leaf_basis, transfer, ranks, out_basis):
    leaves, rank_cap, wide = leaf_basis.shape
    points = wide // 2
    columns = rhs.shape[1]
    levels = transfer.shape[0]
    chunk_leaves = leaves // SLOTS
    half = chunk_leaves // 2
    owned = leaves // lax.axis_size("col")
    in_vmem = lambda array: pltpu.with_memory_space_constraint(array, pltpu.VMEM)
    in_hbm = lambda array: pltpu.with_memory_space_constraint(array, pltpu.HBM)
    sources = in_hbm(rhs.reshape(chunk_leaves, SLOTS, points, columns))
    bases = in_hbm(leaf_basis.reshape(chunk_leaves, SLOTS, rank_cap, wide))
    transfers = in_hbm(transfer.reshape(levels, leaves, rank_cap, 4 * rank_cap))
    half_out = ((half, rank_cap, columns), jnp.float32)
    level_out = ((leaves, rank_cap, 4 * rank_cap), transfer.dtype)

    def run(name, body, arrays, outs, token, scratch=(), from_hbm=False, last=False):
        token = token if isinstance(token, tuple) else (token,)
        vmem = pl.BlockSpec(memory_space=pltpu.VMEM)
        anywhere = pl.BlockSpec(memory_space=pl.ANY)
        if not from_hbm:
            arrays = [in_vmem(array) for array in arrays]
        return pl.pallas_call(
            functools.partial(kernel, body=body, first=len(token), ins=len(arrays)),
            in_specs=[anywhere] * len(token) + [anywhere if from_hbm else vmem] * len(arrays),
            out_specs=[vmem] * len(outs),
            out_shape=[jax.ShapeDtypeStruct(*out) if last else pltpu.VMEM(*out) for out in outs],
            scratch_shapes=scratch,
            cost_estimate=pl.CostEstimate(flops=1 << 33, bytes_accessed=1 << 20, transcendentals=0),
            compiler_params=pltpu.CompilerParams(vmem_limit_bytes=16 * 1024 * 1024),
            name=name,
        )(*token, *arrays)

    token = transfers
    kept, arrived, added, near, offset = {}, {}, {}, {}, {}
    live = far = targets = result = None
    matrices, coming = [], {}
    late = lambda slot: [added[slot, "kept"]] if (slot, "kept") in added else []
    for step in ORDER:
        name = "_".join(str(part) for part in step[:3])
        if step[0] == "first":
            scratch = [
                pltpu.VMEM((2, half, points, columns), rhs.dtype),
                pltpu.VMEM((2, half, rank_cap, wide), leaf_basis.dtype),
                pltpu.SemaphoreType.DMA((4,)),
            ]
            body = functools.partial(first_body, half=half)
            sent, kept[0] = run(name, body, [sources, bases], [half_out] * 2, token, scratch, True)
            arrived[0] = {"sent": swap(sent, "row", 1)}
            offset[0] = 0
            token = kept[0]
        elif step[0] == "tables":
            scratch = [pltpu.VMEM(ranks.shape, ranks.dtype), pltpu.SemaphoreType.DMA((2,))]
            outs = [((levels, leaves, columns), jnp.int32), level_out]
            live, made = run(name, tables_body, [transfers, in_hbm(ranks)], outs, token, scratch, True)
            matrices.append(made)
            token = live
        elif step[0] == "rest":
            scratch = [
                pltpu.VMEM((SLOTS - 1, chunk_leaves, points, columns), rhs.dtype),
                pltpu.VMEM((SLOTS - 1, chunk_leaves, rank_cap, wide), leaf_basis.dtype),
                pltpu.SemaphoreType.DMA((2 * SLOTS,)),
            ]
            outs = [(((SLOTS - 1) * half, rank_cap, columns), jnp.float32)] * 2 + [level_out]
            body = functools.partial(rest_body, half=half)
            sent, token, made = run(name, body, [sources, bases, transfers], outs, token, scratch, True)
            matrices.append(made)
            sent = {"sent": swap(sent, "row", 1)}
            for slot in range(1, SLOTS):
                kept[slot], arrived[slot], offset[slot] = token, sent, (slot - 1) * half
        elif step[0] == "load":
            scratch = [pltpu.SemaphoreType.DMA((levels - 2,))]
            matrices += run(name, load_body, [transfers], [level_out] * (levels - 2), token, scratch, True)
            token = matrices[-1]
        elif step[0] == "targets":
            outs = [((owned, points, 2 * rank_cap), out_basis.dtype)]
            (targets,) = run(name, targets_body, [in_hbm(out_basis)], outs, token, [pltpu.SemaphoreType.DMA], True)
            token = targets
        elif step[0] == "mix":
            level, slot, pieces = step[1:4]
            if step[4:]:
                token = (token, arrived[step[4]]["sent"])
            last = level == levels - 1
            in_parts = "sent" not in arrived[slot]
            partner = arrived[slot]["sent_a" if pieces == ("sent",) else "sent_b"] if in_parts else arrived[slot]["sent"]
            body = functools.partial(
                mix_body, level=level, slot=slot, pieces=pieces, half=half, offset=offset[slot], in_parts=in_parts
            )
            plus = [added[slot, "sent"]] if last and slot % 2 and "sent" in pieces else []
            counts = {"kept_sent": 2 * half, "sent_a": half // 2, "sent_b": half // 2}
            outs = [((counts.get(piece, half), rank_cap, columns), jnp.float32) for piece in pieces]
            made = dict(zip(pieces, run(name, body, [live, matrices[level], kept[slot], partner] + plus, outs, token)))
            token = made[pieces[-1]]
            if last and slot % 2 == 0:
                for piece, other in (("kept", "sent"), ("sent", "kept"), ("kept_sent", "sent")):
                    if piece in made:
                        added[slot + 1, other] = swap(made[piece], "col", 3)
            elif last:
                if "sent" in made:
                    near[slot] = swap(made["sent"], "col", 1)
                if "kept" in made:
                    kept[slot] = made["kept"]
            else:
                coming.setdefault((level, slot), {}).update(
                    {piece: swap(made[piece], "row", 2 << level) for piece in pieces if piece != "kept"}
                )
                if "kept" in made:
                    kept[slot], arrived[slot], offset[slot] = made["kept"], coming[level, slot], 0
        elif step[0] == "far":
            (token,) = run(name, far_body, [kept[1], near[1]] + late(1), [half_out], token)
            far = swap(token, "col", 4)
        else:
            out = ((owned * points, columns), jnp.bfloat16)
            arrays = [targets, kept[3], near[3], far] + late(3)
            (result,) = run(name, end_body, arrays, [out], token, last=True)
    return result


def solution(mesh):
    in_specs = (
        P(("row", "col"), None),
        P(("row", "col"), None, None),
        P(None, "row", "col", None, None, None),
        P(None, "row", "col", None),
        P("row", None, None, None),
    )
    out_specs = P(("row", "col"), None)
    return jax.shard_map(shards, mesh=mesh, in_specs=in_specs, out_specs=out_specs, check_vma=False)
```

```python
import functools

import jax
import jax.numpy as jnp
from jax import lax
from jax.experimental import pallas as pl
from jax.experimental.pallas import tpu as pltpu
from jax.sharding import PartitionSpec as P

SLOTS = 4
LEVELS = 4

ORDER = [
    ('first',),
    ('tables',),
    ('mix', 0, 0, ('sent', 'kept')),
    ('rest',),
    ('load',),
    ('mix', 0, 1, ('sent', 'kept')),
    ('mix', 1, 0, ('sent', 'kept')),
    ('mix', 1, 1, ('sent', 'kept')),
    ('mix', 0, 2, ('sent', 'kept')),
    ('mix', 2, 0, ('sent', 'kept')),
    ('mix', 1, 2, ('sent_a', 'sent_b', 'kept')),
    ('mix', 0, 3, ('sent', 'kept')),
    ('mix', 2, 1, ('sent', 'kept')),
    ('mix', 3, 0, ('kept_sent',)),
    ('mix', 3, 1, ('sent', 'kept')),
    ('mix', 2, 2, ('sent',)),
    ('mix', 1, 3, ('sent', 'kept')),
    ('mix', 2, 2, ('kept',)),
    ('mix', 3, 2, ('kept_sent',)),
    ('mix', 2, 3, ('sent', 'kept')),
    ('far',),
    ('targets',),
    ('mix', 3, 3, ('sent', 'kept')),
    ('end',),
]


def swap(block, axis, mask):
    count = lax.axis_size(axis)
    return lax.ppermute(block, axis, [(at, at ^ mask) for at in range(count)])


def turn(block):
    middle = block.shape[-1] // 2
    return jnp.concatenate([-block[:, middle:], block[:, :middle]], -1)


def split(block):
    high = block.astype(jnp.bfloat16)
    low = (block - high.astype(jnp.float32)).astype(jnp.bfloat16)
    return high, low


def stack_split(blocks):
    highs, lows = [], []
    for block in blocks:
        high, low = split(block)
        highs += [high, turn(high)]
        lows += [low, turn(low)]
    return jnp.concatenate([jnp.concatenate(highs, 0), jnp.concatenate(lows, 0)], 1)


def halves(bit, half):
    return (1 - bit) * half, bit * half


def piece_range(piece, level, half):
    bit = owner_bit() if level == LEVELS - 1 else level_bit(level + 1)
    sent, kept = halves(bit, half)
    if piece == "kept":
        return kept, half
    if piece == "sent":
        return sent, half
    first, second = halves(level_bit(level + 2), half // 2)
    return sent + (first if piece == "sent_a" else second), half // 2


def slot_chunk(slot):
    return (lax.axis_index("col") >> 1) ^ (SLOTS - 1 - slot)


def leaf_product(source, basis):
    stacked = jnp.concatenate([source, turn(source)], 0)
    return jnp.dot(basis, stacked, preferred_element_type=jnp.float32)


def first_body(mine, outs, *, half):
    rhs_ref, basis_ref = mine
    sent_ref, kept_ref, rhs_to, basis_to, sems = outs
    chunk = slot_chunk(0)
    starts = halves(level_bit(0), half)
    loads = []
    for which, start in enumerate(starts):
        for array, to in ((rhs_ref, rhs_to), (basis_ref, basis_to)):
            load = pltpu.make_async_copy(array.at[pl.ds(start, half), chunk], to.at[which], sems.at[len(loads)])
            load.start()
            loads.append(load)
    for which, out_ref in enumerate((sent_ref, kept_ref)):
        loads[2 * which].wait()
        loads[2 * which + 1].wait()
        for at in range(half):
            out_ref[at] = leaf_product(rhs_to[which, at], basis_to[which, at])


def tables_body(mine, outs):
    matrices_ref, ranks_ref = mine
    live_ref, matrices_to, ranks_to, sems = outs
    ranks_load = pltpu.make_async_copy(ranks_ref, ranks_to, sems.at[0])
    ranks_load.start()
    matrices_load = pltpu.make_async_copy(matrices_ref.at[0], matrices_to, sems.at[1])
    matrices_load.start()
    ranks_load.wait()
    levels, leaves, columns = live_ref.shape
    diagonal = lax.broadcasted_iota(jnp.int32, (leaves, leaves), 0) == lax.broadcasted_iota(jnp.int32, (leaves, leaves), 1)
    for level in range(levels):
        spread = jnp.broadcast_to(ranks_to[level, 0], (leaves, leaves)).astype(jnp.float32)
        column = jnp.sum(jnp.where(diagonal, spread, 0.0), axis=1, keepdims=True)
        live_ref[level] = jnp.broadcast_to(column, (leaves, columns)).astype(jnp.int32)
    matrices_load.wait()


def rest_body(mine, outs, *, half):
    rhs_ref, basis_ref, matrices_ref = mine
    sent_ref, kept_ref, matrices_to, rhs_to, basis_to, sems = outs
    starts = halves(level_bit(0), half)
    loads = []
    for slot in range(1, SLOTS):
        chunk = slot_chunk(slot)
        for at, (array, to) in enumerate(((rhs_ref, rhs_to), (basis_ref, basis_to))):
            load = pltpu.make_async_copy(array.at[:, chunk], to.at[slot - 1], sems.at[2 * slot + at])
            load.start()
            loads.append(load)
    matrices_load = pltpu.make_async_copy(matrices_ref.at[1], matrices_to, sems.at[0])
    matrices_load.start()
    for slot in range(1, SLOTS):
        loads[2 * slot - 2].wait()
        loads[2 * slot - 1].wait()
        for to_ref, start in zip((sent_ref, kept_ref), starts):
            for at in range(half):
                product = leaf_product(rhs_to[slot - 1, start + at], basis_to[slot - 1, start + at])
                to_ref[(slot - 1) * half + at] = product
    matrices_load.wait()


def load_body(mine, outs):
    tos, sems = outs[:-1], outs[-1]
    loads = [
        pltpu.make_async_copy(mine[0].at[level + 2], to, sems.at[level]) for level, to in enumerate(tos)
    ]
    for load in loads:
        load.start()
    for load in loads:
        load.wait()


def targets_body(mine, outs):
    to, sem = outs
    owned = to.shape[0]
    load = pltpu.make_async_copy(mine[0].at[0, pl.ds(lax.axis_index("col") * owned, owned)], to, sem)
    load.start()
    load.wait()


def mix_body(mine, outs, *, level, slot, pieces, half, offset, in_parts):
    live_ref, matrices_ref, own_ref, partner_ref = mine[:4]
    added = mine[4:]
    rank_cap, columns = outs[0].shape[1:]
    low_count = 2 << level
    chunk = slot_chunk(slot)
    rows = lax.broadcasted_iota(jnp.int32, (rank_cap, columns), 0)
    if pieces == ("kept_sent",):
        pieces, outs = ("kept", "sent"), (outs[0].at[pl.ds(0, half)], outs[0].at[pl.ds(half, half)])
    for piece, out_ref in zip(pieces, outs):
        start, count = piece_range(piece, level, half)
        for pair in range(count // 2):
            j = start // 2 + pair
            partner = partner_ref[pair if in_parts else offset + j]
            stacked = stack_split([own_ref[offset + j], partner])
            first = start + 2 * pair
            place = (first // low_count) * (SLOTS * low_count) + chunk * low_count + first % low_count
            left = jnp.concatenate([matrices_ref[place], matrices_ref[place + 1]], 0)
            both = jnp.dot(left, stacked, preferred_element_type=jnp.float32)
            both = both[:, :columns] + both[:, columns:]
            for s in range(2):
                live = live_ref[level, pl.ds(place + s, 1), :]
                mixed = jnp.where(rows < live, both[s * rank_cap : (s + 1) * rank_cap], 0.0)
                if added and added[0].shape[0] > half:
                    mixed = mixed + added[0][(half if piece == "kept" else 0) + 2 * pair + s]
                elif added:
                    mixed = mixed + added[0][2 * pair + s]
                out_ref[2 * pair + s] = mixed


def far_body(mine, outs):
    for at in range(outs[0].shape[0]):
        total = mine[0][at]
        for other in mine[1:]:
            total = total + other[at]
        outs[0][at] = total


def end_body(mine, outs):
    basis_ref, *summed = mine
    out_ref = outs[0]
    points = basis_ref.shape[1]
    columns = out_ref.shape[1]
    for at in range(basis_ref.shape[0]):
        total = summed[0][at]
        for other in summed[1:]:
            total = total + other[at]
        both = jnp.dot(basis_ref[at], stack_split([total]), preferred_element_type=jnp.float32)
        both = both[:, :columns] + both[:, columns:]
        out_ref[at * points : (at + 1) * points, :] = both.astype(out_ref.dtype)


def kernel(*refs, body, first, ins):
    body(refs[first : first + ins], refs[first + ins :])


def level_bit(level):
    return lax.axis_index("row") >> level & 1


def owner_bit():
    return lax.axis_index("col") & 1


def shards(rhs, leaf_basis, transfer, ranks, out_basis):
    leaves, rank_cap, wide = leaf_basis.shape
    points = wide // 2
    columns = rhs.shape[1]
    levels = transfer.shape[0]
    chunk_leaves = leaves // SLOTS
    half = chunk_leaves // 2
    owned = leaves // lax.axis_size("col")
    in_vmem = lambda array: pltpu.with_memory_space_constraint(array, pltpu.VMEM)
    in_hbm = lambda array: pltpu.with_memory_space_constraint(array, pltpu.HBM)
    sources = in_hbm(rhs.reshape(chunk_leaves, SLOTS, points, columns))
    bases = in_hbm(leaf_basis.reshape(chunk_leaves, SLOTS, rank_cap, wide))
    transfers = in_hbm(transfer.reshape(levels, leaves, rank_cap, 4 * rank_cap))
    half_out = ((half, rank_cap, columns), jnp.float32)
    level_out = ((leaves, rank_cap, 4 * rank_cap), transfer.dtype)

    def run(name, body, arrays, outs, token, scratch=(), from_hbm=False, last=False):
        token = token if isinstance(token, tuple) else (token,)
        vmem = pl.BlockSpec(memory_space=pltpu.VMEM)
        anywhere = pl.BlockSpec(memory_space=pl.ANY)
        if not from_hbm:
            arrays = [in_vmem(array) for array in arrays]
        return pl.pallas_call(
            functools.partial(kernel, body=body, first=len(token), ins=len(arrays)),
            in_specs=[anywhere] * len(token) + [anywhere if from_hbm else vmem] * len(arrays),
            out_specs=[vmem] * len(outs),
            out_shape=[jax.ShapeDtypeStruct(*out) if last else pltpu.VMEM(*out) for out in outs],
            scratch_shapes=scratch,
            cost_estimate=pl.CostEstimate(flops=1 << 33, bytes_accessed=1 << 20, transcendentals=0),
            compiler_params=pltpu.CompilerParams(vmem_limit_bytes=16 * 1024 * 1024),
            name=name,
        )(*token, *arrays)

    token = transfers
    kept, arrived, added, near, offset = {}, {}, {}, {}, {}
    live = far = targets = result = None
    matrices, coming = [], {}
    late = lambda slot: [added[slot, "kept"]] if (slot, "kept") in added else []
    for step in ORDER:
        name = "_".join(str(part) for part in step[:3])
        if step[0] == "first":
            scratch = [
                pltpu.VMEM((2, half, points, columns), rhs.dtype),
                pltpu.VMEM((2, half, rank_cap, wide), leaf_basis.dtype),
                pltpu.SemaphoreType.DMA((4,)),
            ]
            body = functools.partial(first_body, half=half)
            sent, kept[0] = run(name, body, [sources, bases], [half_out] * 2, token, scratch, True)
            arrived[0] = {"sent": swap(sent, "row", 1)}
            offset[0] = 0
            token = kept[0]
        elif step[0] == "tables":
            scratch = [pltpu.VMEM(ranks.shape, ranks.dtype), pltpu.SemaphoreType.DMA((2,))]
            outs = [((levels, leaves, columns), jnp.int32), level_out]
            live, made = run(name, tables_body, [transfers, in_hbm(ranks)], outs, token, scratch, True)
            matrices.append(made)
            token = live
        elif step[0] == "rest":
            scratch = [
                pltpu.VMEM((SLOTS - 1, chunk_leaves, points, columns), rhs.dtype),
                pltpu.VMEM((SLOTS - 1, chunk_leaves, rank_cap, wide), leaf_basis.dtype),
                pltpu.SemaphoreType.DMA((2 * SLOTS,)),
            ]
            outs = [(((SLOTS - 1) * half, rank_cap, columns), jnp.float32)] * 2 + [level_out]
            body = functools.partial(rest_body, half=half)
            sent, token, made = run(name, body, [sources, bases, transfers], outs, token, scratch, True)
            matrices.append(made)
            sent = {"sent": swap(sent, "row", 1)}
            for slot in range(1, SLOTS):
                kept[slot], arrived[slot], offset[slot] = token, sent, (slot - 1) * half
        elif step[0] == "load":
            scratch = [pltpu.SemaphoreType.DMA((levels - 2,))]
            matrices += run(name, load_body, [transfers], [level_out] * (levels - 2), token, scratch, True)
            token = matrices[-1]
        elif step[0] == "targets":
            outs = [((owned, points, 2 * rank_cap), out_basis.dtype)]
            (targets,) = run(name, targets_body, [in_hbm(out_basis)], outs, token, [pltpu.SemaphoreType.DMA], True)
            token = targets
        elif step[0] == "mix":
            level, slot, pieces = step[1:4]
            if step[4:]:
                token = (token, arrived[step[4]]["sent"])
            last = level == levels - 1
            in_parts = "sent" not in arrived[slot]
            partner = arrived[slot]["sent_a" if pieces == ("sent",) else "sent_b"] if in_parts else arrived[slot]["sent"]
            body = functools.partial(
                mix_body, level=level, slot=slot, pieces=pieces, half=half, offset=offset[slot], in_parts=in_parts
            )
            plus = [added[slot, "sent"]] if last and slot % 2 and "sent" in pieces else []
            counts = {"kept_sent": 2 * half, "sent_a": half // 2, "sent_b": half // 2}
            outs = [((counts.get(piece, half), rank_cap, columns), jnp.float32) for piece in pieces]
            made = dict(zip(pieces, run(name, body, [live, matrices[level], kept[slot], partner] + plus, outs, token)))
            token = made[pieces[-1]]
            if last and slot % 2 == 0:
                for piece, other in (("kept", "sent"), ("sent", "kept"), ("kept_sent", "sent")):
                    if piece in made:
                        added[slot + 1, other] = swap(made[piece], "col", 3)
            elif last:
                if "sent" in made:
                    near[slot] = swap(made["sent"], "col", 1)
                if "kept" in made:
                    kept[slot] = made["kept"]
            else:
                coming.setdefault((level, slot), {}).update(
                    {piece: swap(made[piece], "row", 2 << level) for piece in pieces if piece != "kept"}
                )
                if "kept" in made:
                    kept[slot], arrived[slot], offset[slot] = made["kept"], coming[level, slot], 0
        elif step[0] == "far":
            (token,) = run(name, far_body, [kept[1], near[1]] + late(1), [half_out], token)
            far = swap(token, "col", 4)
        else:
            out = ((owned * points, columns), jnp.bfloat16)
            arrays = [targets, kept[3], near[3], far] + late(3)
            (result,) = run(name, end_body, arrays, [out], token, last=True)
    return result


def solution(mesh):
    in_specs = (
        P(("row", "col"), None),
        P(("row", "col"), None, None),
        P(None, "row", "col", None, None, None),
        P(None, "row", "col", None),
        P("row", None, None, None),
    )
    out_specs = P(("row", "col"), None)
    return jax.shard_map(shards, mesh=mesh, in_specs=in_specs, out_specs=out_specs, check_vma=False)
```
